256 devices in a mesh: dp: 16 (over x, y), tensor: 16 (over z, core).
Axes of the slice: x: 4, y: 4, z: 8, core: 2. Of those that a mesh axis runs over, the one named last changes fastest.
Arguments:
- tokens: bfloat16 [8192, 7424], P(('dp', 'tensor')), may hold values from -6 to 6
- out_grad: bfloat16 [8192, 7424], P(('dp', 'tensor')), may hold values from -6 to 6
- gate_pre: bfloat16 [8192, 29696], P('dp', 'tensor'), may hold values from -8 to 8
- up_pre: bfloat16 [8192, 29696], P('dp', 'tensor'), may hold values from -6 to 6
- hidden_grad: bfloat16 [8192, 29696], P('dp', 'tensor'), may hold values from -6 to 6
- warm_basis: bfloat16 [3, 64, 29696], P(None, None, 'tensor'), may hold values from -0.03125 to 0.03125
Outputs:
- factor_left: float32 [3, 64, 7424], P(None, None, 'tensor')
- factor_right: float32 [3, 64, 29696], P(None, None, 'tensor')
The draws below stay inside these ranges and needn't reach their ends.
All inputs are finite; a program needn't handle non-finite values.
Results may differ from the reference program's by a relative error of at most 0.0048.
Values may be sent and summed in bfloat16 or wider, within the bound.
A program may use at most 128 MiB of HBM per device.

```python
import jax
import jax.numpy as jnp
from jax import lax

D = 7424
FF = 29696
RANK = 64
TOK_DP = 512
TOKENS = 8192
N_DP = 16


def levels(own_key, shape, shards, least, largest):
    gain, own = 1.0, jax.random.fold_in(own_key, 6)
    for dim, parts in shards:
        heights = jnp.exp(jax.random.uniform(jax.random.fold_in(own, dim), (parts,), jnp.float32, least / len(shards), largest / len(shards)))
        gain = gain * jnp.repeat(heights, shape[dim] // parts).reshape([-1 if axis == dim else 1 for axis in range(len(shape))])
    return gain


def gaussian(key, shape, scale, limit, shards=(), kind=jnp.bfloat16):
    drawn = scale * jax.random.normal(key, shape, jnp.float32)
    if shards:
        drawn = drawn * levels(key, shape, shards, -0.22, 0.18)
    return jnp.clip(drawn, -limit, limit).astype(kind)


def setup_inputs(seed: int = 0) -> dict:
    splits = jax.random.split(jax.random.key(seed), 7)
    return {
        "tokens": gaussian(splits[0], (TOKENS, D), 1.0, 6.0, ((0, 256),)),
        "out_grad": gaussian(splits[1], (TOKENS, D), 1.0, 6.0, ((0, 256),)),
        "gate_pre": gaussian(splits[2], (TOKENS, FF), 1.5, 8.0, ((0, 16), (1, 16))),
        "up_pre": gaussian(splits[3], (TOKENS, FF), 1.0, 6.0, ((0, 16), (1, 16))),
        "hidden_grad": gaussian(splits[4], (TOKENS, FF), 1.0, 6.0, ((0, 16), (1, 16))),
        "warm_basis": gaussian(splits[5], (3, RANK, FF), FF ** -0.5, 0.03125, ((2, 16),)),
    }


def swiglu_stack(gate_pre, up_pre, hidden_grad):
    gate_value = gate_pre.astype(jnp.float32)
    up_value = up_pre.astype(jnp.float32)
    grad_value = hidden_grad.astype(jnp.float32)
    sigmoid_value = jax.nn.sigmoid(gate_value)
    silu_value = gate_value * sigmoid_value
    silu_slope = sigmoid_value * (1.0 + gate_value * (1.0 - sigmoid_value))
    hidden = (silu_value * up_value).astype(jnp.bfloat16)
    gate_grad = (grad_value * up_value * silu_slope).astype(jnp.bfloat16)
    up_grad = (grad_value * silu_value).astype(jnp.bfloat16)
    return jnp.stack([gate_grad, up_grad, hidden])

def reference(tokens, out_grad, gate_pre, up_pre, hidden_grad, warm_basis):
    highest = lax.Precision.HIGHEST
    group_tokens = tokens.reshape(N_DP, TOK_DP, D)
    group_grads = out_grad.reshape(N_DP, TOK_DP, D)
    group_gate = gate_pre.reshape(N_DP, TOK_DP, FF)
    group_up = up_pre.reshape(N_DP, TOK_DP, FF)
    group_hidden = hidden_grad.reshape(N_DP, TOK_DP, FF)
    basis = warm_basis.astype(jnp.float32)

    def stacks(items):
        right_side = swiglu_stack(items[2], items[3], items[4]).astype(jnp.float32)
        left_side = jnp.stack([items[0], items[0], items[1]]).astype(jnp.float32)
        return (left_side, right_side)

    def left_part(items):
        left_side, right_side = stacks(items)
        coeff = jnp.einsum('ktf,krf->ktr', right_side, basis, precision=highest)
        return jnp.einsum('ktr,ktd->krd', coeff, left_side, precision=highest)
    every = (group_tokens, group_grads, group_gate, group_up, group_hidden)
    left_sum = jnp.sum(lax.map(left_part, every), axis=0)
    gram_matrix = jnp.einsum('krd,ksd->krs', left_sum, left_sum, precision=highest)
    lower_factor = jnp.linalg.cholesky(gram_matrix)
    factor_left = lax.linalg.triangular_solve(lower_factor, left_sum, left_side=True, lower=True)

    def right_part(items):
        left_side, right_side = stacks(items)
        proj = jnp.einsum('krd,ktd->krt', factor_left, left_side, precision=highest)
        proj = proj.astype(jnp.bfloat16).astype(jnp.float32)
        return jnp.einsum('krt,ktf->krf', proj, right_side, precision=highest)
    factor_right = jnp.sum(lax.map(right_part, every), axis=0) / N_DP
    return (factor_left, factor_right)
```

```python
import functools

import jax
import jax.numpy as jnp
from jax import lax
from jax.experimental import pallas as pl
from jax.experimental.pallas import tpu as pltpu
from jax.sharding import PartitionSpec as P

MESH = pl.DeviceIdType.MESH
F32 = jnp.float32
BF16 = jnp.bfloat16
HIGHEST = lax.Precision.HIGHEST

ROWS = 32
DW = 464
DWP = 512
FFW = 1856
GROUP = 512
CHUNK = 128
NCHUNK = GROUP // CHUNK
LANE_BLOCKS = ((0, 512), (512, 512), (1024, 512), (1536, 320))


def dot(a, b, dims, precision=None):
    return lax.dot_general(a, b, (dims, ((), ())), precision=precision, preferred_element_type=F32)


NN = ((1,), (0,))
NT = ((1,), (1,))


def split(value):
    high = value.astype(BF16)
    return high, (value - high.astype(F32)).astype(BF16)


def kernel(
    tok_hbm, og_hbm, gate_hbm, up_hbm, hid_hbm, warm_hbm,
    out_left, out_right,
    tok, og, gate, up, hid, wp,
    apad, arecv, bmat, cpart, csib, csum, crecv, cgath,
    lpart, lsib, lsum, lrecv, lfull,
    upart, urecv, gpart, grecv, gfull,
    pown, pgath, lown, lout,
    rpart, rrecv, rown, rgath,
    ldma, cdma, ssem, rsem,
):
    dp = lax.axis_index("dp")
    t = lax.axis_index("tensor")
    x, y = dp // 4, dp % 4
    z, c = t // 2, t % 2

    def d_peer(d):
        return ((x + d // 4) % 4) * 4 + (y + d % 4) % 4

    def d_back(d):
        return ((x + 4 - d // 4) % 4) * 4 + (y + 4 - d % 4) % 4

    def z_peer(d):
        return (z + d) % 8

    def remote(src, dst, i, device):
        return pltpu.make_async_remote_copy(
            src, dst, ssem.at[i], rsem.at[i], device_id=device, device_id_type=MESH
        )

    def arrived(ref, i):
        pltpu.make_async_copy(ref, ref, rsem.at[i]).wait()

    def sent(ref, i):
        pltpu.make_async_copy(ref, ref, ssem.at[i]).wait()

    def each(n, body):
        def step(i, carry):
            body(i)
            return carry
        lax.fori_loop(1, n, step, 0)

    barrier = pltpu.get_barrier_semaphore()
    each(16, lambda d: pl.semaphore_signal(barrier, inc=1, device_id=(d_peer(d), t), device_id_type=MESH))
    each(16, lambda d: pl.semaphore_signal(barrier, inc=1, device_id=(dp, (t + d) % 16), device_id_type=MESH))

    copies = [
        pltpu.make_async_copy(tok_hbm, tok, ldma.at[0]),
        pltpu.make_async_copy(og_hbm, og, ldma.at[1]),
        pltpu.make_async_copy(warm_hbm.at[0], wp.at[0, pl.ds(0, 64)], ldma.at[2]),
        pltpu.make_async_copy(warm_hbm.at[1], wp.at[1, pl.ds(64, 64)], ldma.at[3]),
        pltpu.make_async_copy(warm_hbm.at[2], wp.at[2, pl.ds(0, 64)], ldma.at[4]),
        pltpu.make_async_copy(warm_hbm.at[2], wp.at[2, pl.ds(64, 64)], ldma.at[5]),
    ]
    for copy in copies:
        copy.start()
    chunk_copies = []
    for ch in range(NCHUNK):
        rows = pl.ds(ch * CHUNK, CHUNK)
        group = [
            pltpu.make_async_copy(src.at[rows], dst.at[rows], cdma.at[i, ch])
            for i, (src, dst) in enumerate(((gate_hbm, gate), (up_hbm, up), (hid_hbm, hid)))
        ]
        for copy in group:
            copy.start()
        chunk_copies.append(group)
    wp[0, 64:128, :] = jnp.zeros((64, FFW), BF16)
    wp[1, 0:64, :] = jnp.zeros((64, FFW), BF16)

    copies[0].wait()
    copies[1].wait()
    keep = lax.broadcasted_iota(jnp.int32, (ROWS, DWP), 1) < DW
    for which, ref in enumerate((tok, og)):
        for g in range(16):
            first = (DW * g) // 128
            shift = DW * g - 128 * first
            width = 512 if shift <= 48 else 640
            wide = ref[:, 128 * first : 128 * first + width].astype(F32)
            if shift:
                wide = pltpu.roll(wide, width - shift, 1)
            apad[which, g] = jnp.where(keep, wide[:, :DWP], 0.0).astype(BF16)
    for copy in copies[2:]:
        copy.wait()

    lane = lax.broadcasted_iota(jnp.int32, (16, 128), 1)
    for ch in range(NCHUNK):
        if ch == 2:
            pl.semaphore_wait(barrier, 30)

            def scatter_tokens(d):
                for which in range(2):
                    remote(apad.at[which, d_peer(d)], arecv.at[which, d], which, (d_peer(d), t)).start()

            each(16, scatter_tokens)
        for copy in chunk_copies[ch]:
            copy.wait()

        def swiglu(i, carry):
            rows = pl.ds(pl.multiple_of(ch * CHUNK + i * 16, 16), 16)
            for start, width in LANE_BLOCKS:
                cols = pl.ds(start, width)
                g = gate[rows, cols].astype(F32)
                u = up[rows, cols].astype(F32)
                h = hid[rows, cols].astype(F32)
                s = 0.5 * jnp.tanh(0.5 * g) + 0.5
                silu = g * s
                slope = s * (1.0 + g * (1.0 - s))
                bmat[0, rows, cols] = (h * u * slope).astype(BF16)
                bmat[1, rows, cols] = (h * silu).astype(BF16)
                bmat[2, rows, cols] = (silu * u).astype(BF16)
            return carry

        lax.fori_loop(0, CHUNK // 16, swiglu, 0)
        rows = pl.ds(ch * CHUNK, CHUNK)
        c01 = dot(bmat[0, rows, :], wp[0], NT) + dot(bmat[1, rows, :], wp[1], NT)
        c22 = dot(bmat[2, rows, :], wp[2], NT)
        for i in range(CHUNK // ROWS):
            owner = ch * (CHUNK // ROWS) + i
            cpart[owner % 2, owner // 2, 0:32, :] = c01[32 * i : 32 * i + 32]
            cpart[owner % 2, owner // 2, 32:48, :] = jnp.where(
                lane < 64, c22[32 * i : 32 * i + 16], c22[32 * i + 16 : 32 * i + 32]
            )

    sibling = (dp, 2 * z + 1 - c)
    remote(cpart.at[1 - c], csib, 2, sibling).start()
    arrived(csib, 2)
    csum[...] = cpart[c] + csib[...]
    each(8, lambda d: remote(csum.at[z_peer(d)], crecv.at[d], 3, (dp, 2 * z_peer(d) + c)).start())
    arrived(crecv.at[pl.ds(1, 7)], 3)
    total = csum[z]
    for d in range(1, 8):
        total = total + crecv[d]
    cgath[0] = total

    each(16, lambda d: remote(cgath.at[0], cgath.at[d], 4, (d_peer(d), t)).start())
    for which in range(2):
        arecv[which, 0] = apad[which, dp]
        arrived(arecv.at[which, pl.ds(1, 15)], which)
    arrived(cgath.at[pl.ds(1, 15)], 4)

    c01 = cgath[:, 0:32, :].reshape(GROUP, 128)
    fold = cgath[:, 32:48, :].reshape(256, 128)
    other = pltpu.roll(fold, 64, 1)
    c2 = jnp.concatenate([fold.reshape(16, 16, 128), other.reshape(16, 16, 128)], axis=1).reshape(GROUP, 128)
    atok = arecv[0].reshape(GROUP, DWP)
    aog = arecv[1].reshape(GROUP, DWP)
    high, low = split(c01.T)
    left01 = dot(high, atok, NN) + dot(low, atok, NN)
    high, low = split(c2.T[0:64])
    left2 = dot(high, aog, NN) + dot(low, aog, NN)
    for half in range(2):
        cols = slice(256 * half, 256 * half + 256)
        lpart[half, 0:128, :] = left01[:, cols]
        lpart[half, 128:192, :] = left2[:, cols]

    remote(lpart.at[1 - c], lsib, 5, sibling).start()
    arrived(lsib, 5)
    lsum[...] = (lpart[c] + lsib[...]).reshape(8, 24, 256)
    each(8, lambda d: remote(lsum.at[z_peer(d)], lrecv.at[d], 6, (dp, 2 * z_peer(d) + c)).start())
    arrived(lrecv.at[pl.ds(1, 7)], 6)
    total = lsum[z]
    for d in range(1, 8):
        total = total + lrecv[d]
    lfull[c, z] = total
    each(8, lambda d: remote(lfull.at[c, z], lfull.at[c, z], 7, (dp, 2 * z_peer(d) + c)).start())
    arrived(lrecv.at[pl.ds(1, 7)], 7)
    remote(lfull.at[c], lfull.at[c], 8, sibling).start()
    arrived(lsib, 8)

    left = jnp.concatenate([lfull[0].reshape(192, 256), lfull[1].reshape(192, 256)], axis=1)
    left01 = left[0:128]
    left2 = left[128:192]
    left22 = jnp.concatenate([left2, left2], axis=0)

    high, low = split(left01)
    u01 = dot(atok, high, NT) + dot(atok, low, NT)
    high, low = split(left22)
    u22 = (dot(aog, high, NT) + dot(aog, low, NT)).reshape(16, 32, 128)
    upart[:, 0:32, :] = u01.reshape(16, 32, 128)
    lane3 = lax.broadcasted_iota(jnp.int32, (16, 16, 128), 2)
    upart[:, 32:48, :] = jnp.where(lane3 < 64, u22[:, 0:16], u22[:, 16:32])
    each(16, lambda d: remote(upart.at[d], urecv.at[d], 9, (d_back(d), t)).start())

    lane64 = lax.broadcasted_iota(jnp.int32, (64, 128), 1)
    gram01 = dot(left01, left01, NT, HIGHEST)
    gram22 = dot(left2, left22, NT, HIGHEST)
    gpart[0:4] = jnp.where(lane64 < 64, gram01[0:64], gram01[64:128]).reshape(4, 16, 128)
    gpart[4:8] = gram22.reshape(4, 16, 128)
    each(16, lambda d: remote(gpart.at[z], grecv.at[d], 10, (d_peer(d), t)).start())
    arrived(grecv.at[pl.ds(1, 15)], 10)
    total = gpart[z]
    for d in range(1, 16):
        total = total + grecv[d]
    gfull[z] = total
    each(8, lambda d: remote(gfull.at[z], gfull.at[z], 11, (dp, 2 * z_peer(d) + c)).start())
    arrived(grecv.at[pl.ds(1, 7)], 11)

    packed = gfull[...].reshape(128, 128)
    pair = pltpu.roll(packed[0:64], 64, 1)
    row64 = lax.broadcasted_iota(jnp.int32, (64, 128), 0)
    unit = jnp.where(lane64 % 64 == row64, 1.0, 0.0)
    work = [
        jnp.where(lane64 < 64, unit, pair),
        jnp.where(lane64 < 64, pair, unit),
        jnp.where(lane64 < 64, unit, packed[64:128]),
    ]
    place = (64, 0, 64)
    for j in range(63):
        top = (j // 8) * 8
        for k in range(3):
            m = work[k]
            pivot_row = m[j : j + 1, :]
            at = place[k] + j
            scaled = pivot_row * (1.0 / m[j : j + 1, at : at + 1])
            below = m[top:, :]
            column = jnp.where(row64[top:, :] > j, below[:, at : at + 1], 0.0)
            below = below - column * scaled
            work[k] = below if top == 0 else jnp.concatenate([m[:top], below], axis=0)
    inverse = []
    for k in range(3):
        m = work[k]
        diagonal = jnp.sum(jnp.where(lane64 == row64 + place[k], m, 0.0), axis=1, keepdims=True)
        m = m * lax.rsqrt(diagonal)
        inverse.append(jnp.where((lane64 < 64) == (place[k] == 64), m, 0.0))
    bd01 = jnp.concatenate([inverse[0], inverse[1]], axis=0)
    bd22 = jnp.concatenate([inverse[2], pltpu.roll(inverse[2], 64, 1)], axis=0)

    arrived(urecv.at[pl.ds(1, 15)], 9)
    total = upart[0]
    for d in range(1, 16):
        total = total + urecv[d]
    proj = jnp.concatenate(
        [dot(total[0:32], bd01, NT, HIGHEST), dot(total[32:48], bd22, NT, HIGHEST)], axis=0
    ).astype(BF16)
    pgath[c, z] = proj
    each(8, lambda d: remote(pgath.at[c, z], pgath.at[c, z], 12, (dp, 2 * z_peer(d) + c)).start())

    owner_x, owner_y = t // 4, t % 4

    @pl.when(dp == t)
    def _():
        lout[0:128, :] = dot(bd01, left01, NN, HIGHEST).astype(BF16)
        lout[128:192, :] = dot(bd22[0:64], left22, NN, HIGHEST).astype(BF16)
        each(4, lambda d: remote(lout, lout, 14, (((x + d) % 4) * 4 + y, t)).start())

    arrived(pgath.at[c, pl.ds(0, 7)], 12)
    remote(pgath.at[c], pgath.at[c], 13, sibling).start()
    arrived(pgath.at[c], 13)

    whole = jnp.concatenate([pgath[i % 2, i // 2, 0:32, :] for i in range(16)], axis=0).astype(F32)
    parts = []
    for i in range(16):
        fold = pgath[i % 2, i // 2, 32:48, :].astype(F32)
        parts += [fold, pltpu.roll(fold, 64, 1)]
    p01 = whole.T.astype(BF16)
    p2 = jnp.concatenate(parts, axis=0).T.astype(BF16)
    lhs = (p01[0:64], p01[64:128], p2[0:64])
    for j, (start, width) in enumerate(LANE_BLOCKS):
        terms = [dot(lhs[k], bmat[k, :, start : start + width], NN).astype(BF16) for k in range(3)]
        both = jnp.concatenate(terms, axis=0)
        for i in range(4):
            rpart[4 * i + j, :, 0:width] = both[48 * i : 48 * i + 48]
    each(16, lambda d: remote(rpart.at[d_peer(d)], rrecv.at[d], 16, (d_peer(d), t)).start())

    @pl.when(jnp.logical_and(y == owner_y, x != owner_x))
    def _():
        arrived(lout, 14)

    @pl.when(y == owner_y)
    def _():
        each(4, lambda d: remote(lout, lout, 15, (x * 4 + (y + d) % 4, t)).start())

    arrived(rrecv.at[pl.ds(1, 15)], 16)
    for r in range(3):
        rows = slice(16 * r, 16 * r + 16)
        total = rpart[dp, rows, :].astype(F32)
        for d in range(1, 16):
            total = total + rrecv[d, rows, :].astype(F32)
        rgath[dp, rows, :] = (total * (1.0 / 16)).astype(BF16)
    each(16, lambda d: remote(rgath.at[dp], rgath.at[dp], 17, (d_peer(d), t)).start())

    @pl.when(y != owner_y)
    def _():
        arrived(lout, 15)

    out_left[...] = lout[:, 0:DW].astype(F32)
    arrived(rrecv.at[pl.ds(1, 15)], 17)
    for i in range(4):
        for j, (start, width) in enumerate(LANE_BLOCKS):
            out_right[48 * i : 48 * i + 48, start : start + width] = rgath[4 * i + j, :, 0:width].astype(F32)

    for which in range(2):
        sent(arecv.at[which, pl.ds(1, 15)], which)
    sent(csib, 2)
    sent(crecv.at[pl.ds(1, 7)], 3)
    sent(cgath.at[pl.ds(1, 15)], 4)
    sent(lsib, 5)
    sent(lrecv.at[pl.ds(1, 7)], 6)
    sent(lrecv.at[pl.ds(1, 7)], 7)
    sent(lsib, 8)
    sent(urecv.at[pl.ds(1, 15)], 9)
    sent(grecv.at[pl.ds(1, 15)], 10)
    sent(grecv.at[pl.ds(1, 7)], 11)
    sent(pgath.at[0, pl.ds(0, 7)], 12)
    sent(pgath.at[0], 13)

    @pl.when(dp == t)
    def _():
        each(4, lambda d: sent(lout, 14))

    @pl.when(y == owner_y)
    def _():
        each(4, lambda d: sent(lout, 15))

    sent(rrecv.at[pl.ds(1, 15)], 16)
    sent(rrecv.at[pl.ds(1, 15)], 17)


def shards(tokens, out_grad, gate_pre, up_pre, hidden_grad, warm_basis):
    vmem = pltpu.VMEM
    scratch = [
        vmem((ROWS, 7424), BF16), vmem((ROWS, 7424), BF16),
        vmem((GROUP, FFW), BF16), vmem((GROUP, FFW), BF16), vmem((GROUP, FFW), BF16),
        vmem((3, 128, FFW), BF16),
        vmem((2, 16, ROWS, DWP), BF16), vmem((2, 16, ROWS, DWP), BF16),
        vmem((3, GROUP, FFW), BF16),
        vmem((2, 8, 48, 128), F32), vmem((8, 48, 128), F32), vmem((8, 48, 128), F32),
        vmem((8, 48, 128), F32), vmem((16, 48, 128), F32),
        vmem((2, 192, 256), F32), vmem((192, 256), F32), vmem((8, 24, 256), F32),
        vmem((8, 24, 256), F32), vmem((2, 8, 24, 256), F32),
        vmem((16, 48, 128), F32), vmem((16, 48, 128), F32),
        vmem((8, 16, 128), F32), vmem((16, 16, 128), F32), vmem((8, 16, 128), F32),
        vmem((48, 128), BF16), vmem((2, 8, 48, 128), BF16),
        vmem((192, DWP), BF16), vmem((192, DWP), BF16),
        vmem((16, 48, 512), BF16), vmem((16, 48, 512), BF16),
        vmem((48, 512), BF16), vmem((16, 48, 512), BF16),
        pltpu.SemaphoreType.DMA((6,)), pltpu.SemaphoreType.DMA((3, NCHUNK)),
        pltpu.SemaphoreType.DMA((18,)), pltpu.SemaphoreType.DMA((18,)),
    ]
    left, right = pl.pallas_call(
        kernel,
        out_shape=(jax.ShapeDtypeStruct((192, DW), F32), jax.ShapeDtypeStruct((192, FFW), F32)),
        in_specs=[pl.BlockSpec(memory_space=pl.ANY)] * 6,
        out_specs=(pl.BlockSpec(memory_space=pltpu.VMEM), pl.BlockSpec(memory_space=pltpu.VMEM)),
        scratch_shapes=scratch,
        compiler_params=pltpu.CompilerParams(
            collective_id=0, has_side_effects=True, vmem_limit_bytes=48 * 2**20
        ),
    )(tokens, out_grad, gate_pre, up_pre, hidden_grad, warm_basis)
    return left.reshape(3, 64, DW), right.reshape(3, 64, FFW)


def solution(mesh):
    placed = (
        P(("dp", "tensor"), None),
        P(("dp", "tensor"), None),
        P("dp", "tensor"),
        P("dp", "tensor"),
        P("dp", "tensor"),
        P(None, None, "tensor"),
    )
    return jax.shard_map(
        shards,
        mesh=mesh,
        in_specs=placed,
        out_specs=(P(None, None, "tensor"), P(None, None, "tensor")),
        check_vma=False,
    )
```

```python
import functools

import jax
import jax.numpy as jnp
from jax import lax
from jax.experimental import pallas as pl
from jax.experimental.pallas import tpu as pltpu
from jax.sharding import PartitionSpec as P

MESH = pl.DeviceIdType.MESH
F32 = jnp.float32
BF16 = jnp.bfloat16
HIGHEST = lax.Precision.HIGHEST

ROWS = 32
DW = 464
DWP = 512
FFW = 1856
GROUP = 512
SPLITS = 2
PIECE = 2048 // (4 * SPLITS)
HALVES = tuple((4 * PIECE * h, min(4 * PIECE, FFW - 4 * PIECE * h)) for h in range(SPLITS))
BLOCKS = ((0, 512), (512, 512), (1024, 512), (1536, 320))


def dot(a, b, dims, precision=None):
    return lax.dot_general(a, b, (dims, ((), ())), precision=precision, preferred_element_type=F32)


NN = ((1,), (0,))
NT = ((1,), (1,))


def split(value):
    high = value.astype(BF16)
    return high, (value - high.astype(F32)).astype(BF16)


def kernel(
    tok_hbm, og_hbm, gate_hbm, up_hbm, hid_hbm, warm_hbm,
    out_left, out_right,
    tok, og, gate, up, hid, warm,
    apad, arecv, bmat, cpart, csib, csum, crecv, cgath,
    lpart, lsib, lsum, lrecv, lfull,
    upart, urecv, gpart, grecv, gfull,
    pgath, lout, rpart, rrecv, rgath,
    ldma, cdma, ssem, rsem,
):
    dp = lax.axis_index("dp")
    t = lax.axis_index("tensor")
    x, y = dp // 4, dp % 4
    z, c = t // 2, t % 2

    def d_peer(d):
        return ((x + d // 4) % 4) * 4 + (y + d % 4) % 4

    def d_back(d):
        return ((x + 4 - d // 4) % 4) * 4 + (y + 4 - d % 4) % 4

    def z_peer(d):
        return (z + d) % 8

    def remote(src, dst, i, device):
        return pltpu.make_async_remote_copy(
            src, dst, ssem.at[i], rsem.at[i], device_id=device, device_id_type=MESH
        )

    def arrived(ref, i):
        pltpu.make_async_copy(ref, ref, rsem.at[i]).wait()

    def sent(ref, i):
        pltpu.make_async_copy(ref, ref, ssem.at[i]).wait()

    def each(n, body):
        def step(i, carry):
            body(i)
            return carry
        lax.fori_loop(1, n, step, 0)

    barrier = pltpu.get_barrier_semaphore()
    each(16, lambda d: pl.semaphore_signal(barrier, inc=1, device_id=(d_peer(d), t), device_id_type=MESH))
    each(16, lambda d: pl.semaphore_signal(barrier, inc=1, device_id=(dp, (t + d) % 16), device_id_type=MESH))

    copies = [
        pltpu.make_async_copy(tok_hbm, tok, ldma.at[0]),
        pltpu.make_async_copy(og_hbm, og, ldma.at[1]),
        pltpu.make_async_copy(warm_hbm, warm, ldma.at[2]),
    ]
    for copy in copies:
        copy.start()
    chunk_copies = []
    for ch, (start, width) in enumerate(BLOCKS):
        rows = pl.ds(start, width)
        group = [
            pltpu.make_async_copy(src.at[rows], dst.at[rows], cdma.at[i, ch])
            for i, (src, dst) in enumerate(((gate_hbm, gate), (up_hbm, up), (hid_hbm, hid)))
        ]
        for copy in group:
            copy.start()
        chunk_copies.append(group)

    copies[0].wait()
    copies[1].wait()
    keep = lax.broadcasted_iota(jnp.int32, (ROWS, DWP), 1) < DW
    for which, ref in enumerate((tok, og)):
        for g in range(16):
            first = (DW * g) // 128
            shift = DW * g - 128 * first
            width = 512 if shift <= 48 else 640
            wide = ref[:, 128 * first : 128 * first + width].astype(F32)
            if shift:
                wide = pltpu.roll(wide, width - shift, 1)
            apad[which, g] = jnp.where(keep, wide[:, :DWP], 0.0).astype(BF16)
    for copy in copies[2:]:
        copy.wait()

    lane = lax.broadcasted_iota(jnp.int32, (16, 128), 1)
    terms = [0.0, 0.0, 0.0]
    for ch, (start, width) in enumerate(BLOCKS):
        if ch == 2:
            pl.semaphore_wait(barrier, 30)

            def scatter_tokens(d):
                for which in range(2):
                    remote(apad.at[which, d_peer(d)], arecv.at[which, d], which, (d_peer(d), t)).start()

            each(16, scatter_tokens)
        for copy in chunk_copies[ch]:
            copy.wait()

        def swiglu(i, carry):
            rows = pl.ds(pl.multiple_of(start + i * 16, 16), 16)
            g = gate[rows, :].astype(F32)
            u = up[rows, :].astype(F32)
            h = hid[rows, :].astype(F32)
            s = 0.5 * jnp.tanh(0.5 * g) + 0.5
            silu = g * s
            slope = s * (1.0 + g * (1.0 - s))
            bmat[0, rows, :] = (h * u * slope).astype(BF16)
            bmat[1, rows, :] = (h * silu).astype(BF16)
            bmat[2, rows, :] = (silu * u).astype(BF16)
            return carry

        lax.fori_loop(0, width // 16, swiglu, 0, unroll=2)
        for k in range(3):
            terms[k] += dot(warm[k, :, start : start + width], bmat[k, start : start + width, :], NN)
    c01 = jnp.concatenate([terms[0], terms[1]], axis=0).T
    c22 = jnp.concatenate([terms[2], terms[2]], axis=0).T
    for i in range(16):
        cpart[i % 2, i // 2, 0:32, :] = c01[32 * i : 32 * i + 32]
        cpart[i % 2, i // 2, 32:48, :] = jnp.where(
            lane < 64, c22[32 * i : 32 * i + 16], c22[32 * i + 16 : 32 * i + 32]
        )

    sibling = (dp, 2 * z + 1 - c)
    remote(cpart.at[1 - c], csib, 2, sibling).start()
    arrived(csib, 2)
    csum[...] = cpart[c] + csib[...]
    each(8, lambda d: remote(csum.at[z_peer(d)], crecv.at[d], 3, (dp, 2 * z_peer(d) + c)).start())
    arrived(crecv.at[pl.ds(1, 7)], 3)
    total = csum[z]
    for d in range(1, 8):
        total = total + crecv[d]
    cgath[0] = total

    each(16, lambda d: remote(cgath.at[0], cgath.at[d], 4, (d_peer(d), t)).start())
    for which in range(2):
        arecv[which, 0] = apad[which, dp]
        arrived(arecv.at[which, pl.ds(1, 15)], which)
    arrived(cgath.at[pl.ds(1, 15)], 4)

    c01 = cgath[:, 0:32, :].reshape(GROUP, 128)
    fold = cgath[:, 32:48, :].reshape(256, 128)
    other = pltpu.roll(fold, 64, 1)
    c2 = jnp.concatenate([fold.reshape(16, 16, 128), other.reshape(16, 16, 128)], axis=1).reshape(GROUP, 128)
    atok = arecv[0].reshape(GROUP, DWP)
    aog = arecv[1].reshape(GROUP, DWP)
    high, low = split(c01.T)
    left01 = dot(high, atok, NN) + dot(low, atok, NN)
    high, low = split(c2.T[0:64])
    left2 = dot(high, aog, NN) + dot(low, aog, NN)
    for half in range(2):
        cols = slice(256 * half, 256 * half + 256)
        lpart[half, 0:128, :] = left01[:, cols]
        lpart[half, 128:192, :] = left2[:, cols]

    remote(lpart.at[1 - c], lsib, 5, sibling).start()
    arrived(lsib, 5)
    lsum[...] = (lpart[c] + lsib[...]).reshape(8, 24, 256)
    each(8, lambda d: remote(lsum.at[z_peer(d)], lrecv.at[d], 6, (dp, 2 * z_peer(d) + c)).start())
    arrived(lrecv.at[pl.ds(1, 7)], 6)
    total = lsum[z]
    for d in range(1, 8):
        total = total + lrecv[d]
    lfull[c, z] = total
    each(8, lambda d: remote(lfull.at[c, z], lfull.at[c, z], 7, (dp, 2 * z_peer(d) + c)).start())
    arrived(lrecv.at[pl.ds(1, 7)], 7)
    remote(lfull.at[c], lfull.at[c], 8, sibling).start()
    arrived(lsib, 8)

    left = jnp.concatenate([lfull[0].reshape(192, 256), lfull[1].reshape(192, 256)], axis=1)
    left01 = left[0:128]
    left2 = left[128:192]
    left22 = jnp.concatenate([left2, left2], axis=0)

    lane64 = lax.broadcasted_iota(jnp.int32, (64, 128), 1)
    gram01 = dot(left01, left01, NT, HIGHEST)
    gram22 = dot(left2, left22, NT, HIGHEST)
    gpart[0:4] = jnp.where(lane64 < 64, gram01[0:64], gram01[64:128]).reshape(4, 16, 128)
    gpart[4:8] = gram22.reshape(4, 16, 128)
    each(16, lambda d: remote(gpart.at[z], grecv.at[d], 10, (d_peer(d), t)).start())

    high, low = split(left01)
    u01 = dot(atok, high, NT) + dot(atok, low, NT)
    high, low = split(left22)
    u22 = (dot(aog, high, NT) + dot(aog, low, NT)).reshape(16, 32, 128)
    upart[:, 0:32, :] = u01.reshape(16, 32, 128)
    lane3 = lax.broadcasted_iota(jnp.int32, (16, 16, 128), 2)
    upart[:, 32:48, :] = jnp.where(lane3 < 64, u22[:, 0:16], u22[:, 16:32])
    each(16, lambda d: remote(upart.at[d], urecv.at[d], 9, (d_back(d), t)).start())

    arrived(grecv.at[pl.ds(1, 15)], 10)
    total = gpart[z]
    for d in range(1, 16):
        total = total + grecv[d]
    gfull[z] = total
    each(8, lambda d: remote(gfull.at[z], gfull.at[z], 11, (dp, 2 * z_peer(d) + c)).start())
    arrived(grecv.at[pl.ds(1, 7)], 11)

    packed = gfull[...].reshape(128, 128)
    pair = pltpu.roll(packed[0:64], 64, 1)
    row64 = lax.broadcasted_iota(jnp.int32, (64, 128), 0)
    unit = jnp.where(lane64 % 64 == row64, 1.0, 0.0)
    work = [
        jnp.where(lane64 < 64, unit, pair),
        jnp.where(lane64 < 64, pair, unit),
        jnp.where(lane64 < 64, unit, packed[64:128]),
    ]
    place = (64, 0, 64)
    for j in range(63):
        top = (j // 8) * 8
        for k in range(3):
            m = work[k]
            pivot_row = m[j : j + 1, :]
            at = place[k] + j
            scaled = pivot_row * (1.0 / m[j : j + 1, at : at + 1])
            below = m[top:, :]
            column = jnp.where(row64[top:, :] > j, below[:, at : at + 1], 0.0)
            below = below - column * scaled
            work[k] = below if top == 0 else jnp.concatenate([m[:top], below], axis=0)
    inverse = []
    for k in range(3):
        m = work[k]
        diagonal = jnp.sum(jnp.where(lane64 == row64 + place[k], m, 0.0), axis=1, keepdims=True)
        m = m * lax.rsqrt(diagonal)
        inverse.append(jnp.where((lane64 < 64) == (place[k] == 64), m, 0.0))
    bd01 = jnp.concatenate([inverse[0], inverse[1]], axis=0)
    bd22 = jnp.concatenate([inverse[2], pltpu.roll(inverse[2], 64, 1)], axis=0)

    arrived(urecv.at[pl.ds(1, 15)], 9)
    total = upart[0]
    for d in range(1, 16):
        total = total + urecv[d]
    proj = jnp.concatenate(
        [dot(total[0:32], bd01, NT, HIGHEST), dot(total[32:48], bd22, NT, HIGHEST)], axis=0
    ).astype(BF16)
    pgath[c, z] = proj
    each(8, lambda d: remote(pgath.at[c, z], pgath.at[c, z], 12, (dp, 2 * z_peer(d) + c)).start())

    owner_x, owner_y = t // 4, t % 4

    @pl.when(dp == t)
    def _():
        lout[0:128, :] = dot(bd01, left01, NN, HIGHEST).astype(BF16)
        lout[128:192, :] = dot(bd22[0:64], left22, NN, HIGHEST).astype(BF16)
        each(4, lambda d: remote(lout, lout, 14, (((x + d) % 4) * 4 + y, t)).start())

    arrived(pgath.at[c, pl.ds(0, 7)], 12)
    remote(pgath.at[c], pgath.at[c], 13, sibling).start()
    arrived(pgath.at[c], 13)

    whole = jnp.concatenate([pgath[i % 2, i // 2, 0:32, :] for i in range(16)], axis=0).astype(F32)
    parts = []
    for i in range(16):
        fold = pgath[i % 2, i // 2, 32:48, :].astype(F32)
        parts += [fold, pltpu.roll(fold, 64, 1)]
    p01 = whole.T.astype(BF16)
    p2 = jnp.concatenate(parts, axis=0).T.astype(BF16)
    lhs = (p01[0:64], p01[64:128], p2[0:64])
    for h, (start, width) in enumerate(HALVES):
        terms = [dot(lhs[k], bmat[k, start : start + width, :], NT).astype(BF16) for k in range(3)]
        both = jnp.concatenate(terms, axis=0)
        for i in range(4):
            for j in range(4):
                size = min(PIECE, width - PIECE * j)
                if size > 0:
                    rpart[h, 4 * i + j, :, 0:size] = both[48 * i : 48 * i + 48, PIECE * j : PIECE * j + size]
        each(16, lambda d: remote(rpart.at[h, d_peer(d)], rrecv.at[h, d], 16 + h, (d_peer(d), t)).start())

    @pl.when(jnp.logical_and(y == owner_y, x != owner_x))
    def _():
        arrived(lout, 14)

    @pl.when(y == owner_y)
    def _():
        each(4, lambda d: remote(lout, lout, 15, (x * 4 + (y + d) % 4, t)).start())

    for h, (start, width) in enumerate(HALVES):
        arrived(rrecv.at[h, pl.ds(1, 15)], 16 + h)
        own_cols = pl.ds(pl.multiple_of(start + y * PIECE, PIECE), PIECE)
        for r in range(3):
            rows = slice(16 * r, 16 * r + 16)
            total = rpart[h, dp, rows, :].astype(F32)
            for d in range(1, 16):
                total = total + rrecv[h, d, rows, :].astype(F32)
            rgath[pl.ds(pl.multiple_of(x * 48 + 16 * r, 16), 16), own_cols] = (total * (1.0 / 16)).astype(BF16)
        own = rgath.at[pl.ds(pl.multiple_of(x * 48, 16), 48), own_cols]
        each(16, lambda d: remote(own, own, 16 + SPLITS + h, (d_peer(d), t)).start())

    @pl.when(y != owner_y)
    def _():
        arrived(lout, 15)

    out_left[...] = lout[:, 0:DW]
    for h, (start, width) in enumerate(HALVES):
        arrived(rrecv.at[h, pl.ds(1, 15)], 16 + SPLITS + h)
        out_right[:, start : start + width] = rgath[:, start : start + width]

    for which in range(2):
        sent(arecv.at[which, pl.ds(1, 15)], which)
    sent(csib, 2)
    sent(crecv.at[pl.ds(1, 7)], 3)
    sent(cgath.at[pl.ds(1, 15)], 4)
    sent(lsib, 5)
    sent(lrecv.at[pl.ds(1, 7)], 6)
    sent(lrecv.at[pl.ds(1, 7)], 7)
    sent(lsib, 8)
    sent(urecv.at[pl.ds(1, 15)], 9)
    sent(grecv.at[pl.ds(1, 15)], 10)
    sent(grecv.at[pl.ds(1, 7)], 11)
    sent(pgath.at[0, pl.ds(0, 7)], 12)
    sent(pgath.at[0], 13)

    @pl.when(dp == t)
    def _():
        each(4, lambda d: sent(lout, 14))

    @pl.when(y == owner_y)
    def _():
        each(4, lambda d: sent(lout, 15))

    for h in range(2 * SPLITS):
        sent(rrecv.at[0, pl.ds(1, 15)], 16 + h)


def shards(tokens, out_grad, gate_pre, up_pre, hidden_grad, warm_basis):
    vmem = pltpu.VMEM
    scratch = [
        vmem((ROWS, 7424), BF16), vmem((ROWS, 7424), BF16),
        vmem((FFW, GROUP), BF16), vmem((FFW, GROUP), BF16), vmem((FFW, GROUP), BF16),
        vmem((3, 64, FFW), BF16),
        vmem((2, 16, ROWS, DWP), BF16), vmem((2, 16, ROWS, DWP), BF16),
        vmem((3, FFW, GROUP), BF16),
        vmem((2, 8, 48, 128), F32), vmem((8, 48, 128), F32), vmem((8, 48, 128), F32),
        vmem((8, 48, 128), F32), vmem((16, 48, 128), F32),
        vmem((2, 192, 256), F32), vmem((192, 256), F32), vmem((8, 24, 256), F32),
        vmem((8, 24, 256), F32), vmem((2, 8, 24, 256), F32),
        vmem((16, 48, 128), F32), vmem((16, 48, 128), F32),
        vmem((8, 16, 128), F32), vmem((16, 16, 128), F32), vmem((8, 16, 128), F32),
        vmem((2, 8, 48, 128), BF16), vmem((192, DWP), BF16),
        vmem((SPLITS, 16, 48, PIECE), BF16), vmem((SPLITS, 16, 48, PIECE), BF16), vmem((192, 2048), BF16),
        pltpu.SemaphoreType.DMA((3,)), pltpu.SemaphoreType.DMA((3, 4)),
        pltpu.SemaphoreType.DMA((16 + 2 * SPLITS,)), pltpu.SemaphoreType.DMA((16 + 2 * SPLITS,)),
    ]
    left, right = pl.pallas_call(
        kernel,
        out_shape=(jax.ShapeDtypeStruct((192, DW), BF16), jax.ShapeDtypeStruct((192, FFW), BF16)),
        in_specs=[pl.BlockSpec(memory_space=pl.ANY)] * 6,
        out_specs=(pl.BlockSpec(memory_space=pltpu.VMEM), pl.BlockSpec(memory_space=pltpu.VMEM)),
        scratch_shapes=scratch,
        compiler_params=pltpu.CompilerParams(
            collective_id=0, has_side_effects=True, vmem_limit_bytes=60 * 2**20
        ),
    )(tokens, out_grad, gate_pre.T, up_pre.T, hidden_grad.T, warm_basis)
    return left.astype(F32).reshape(3, 64, DW), right.astype(F32).reshape(3, 64, FFW)


def solution(mesh):
    placed = (
        P(("dp", "tensor"), None),
        P(("dp", "tensor"), None),
        P("dp", "tensor"),
        P("dp", "tensor"),
        P("dp", "tensor"),
        P(None, None, "tensor"),
    )
    return jax.shard_map(
        shards,
        mesh=mesh,
        in_specs=placed,
        out_specs=(P(None, None, "tensor"), P(None, None, "tensor")),
        check_vma=False,
    )
```

```python
import functools

import jax
import jax.numpy as jnp
from jax import lax
from jax.experimental import pallas as pl
from jax.experimental.pallas import tpu as pltpu
from jax.sharding import PartitionSpec as P

MESH = pl.DeviceIdType.MESH
F32 = jnp.float32
BF16 = jnp.bfloat16
HIGHEST = lax.Precision.HIGHEST

ROWS = 32
DW = 464
DWP = 512
FFW = 1856
GROUP = 512
SPLITS = 2
PIECE = 2048 // (4 * SPLITS)
HALVES = tuple((4 * PIECE * h, min(4 * PIECE, FFW - 4 * PIECE * h)) for h in range(SPLITS))
BLOCKS = ((0, 512), (512, 512), (1024, 512), (1536, 320))


def dot(a, b, dims, precision=None):
    return lax.dot_general(a, b, (dims, ((), ())), precision=precision, preferred_element_type=F32)


NN = ((1,), (0,))
NT = ((1,), (1,))


def split(value):
    high = value.astype(BF16)
    return high, (value - high.astype(F32)).astype(BF16)


def kernel(
    tok_hbm, og_hbm, gate_hbm, up_hbm, hid_hbm, warm_hbm,
    out_left, out_right,
    tok, og, gate, up, hid, warm,
    apad, arecv, bmat, cpart, csib, csum, crecv, cgath,
    lpart, lsib, lsum, lrecv, lfull,
    upart, urecv, gpart, grecv, gfull,
    pgath, lout, rpart, rrecv, rgath,
    ldma, cdma, ssem, rsem,
):
    dp = lax.axis_index("dp")
    t = lax.axis_index("tensor")
    x, y = dp // 4, dp % 4
    z, c = t // 2, t % 2

    def d_peer(d):
        return ((x + d // 4) % 4) * 4 + (y + d % 4) % 4

    def d_back(d):
        return ((x + 4 - d // 4) % 4) * 4 + (y + 4 - d % 4) % 4

    def z_peer(d):
        return (z + d) % 8

    def remote(src, dst, i, device):
        return pltpu.make_async_remote_copy(
            src, dst, ssem.at[i], rsem.at[i], device_id=device, device_id_type=MESH
        )

    def arrived(ref, i):
        pltpu.make_async_copy(ref, ref, rsem.at[i]).wait()

    def sent(ref, i):
        pltpu.make_async_copy(ref, ref, ssem.at[i]).wait()

    def each(n, body):
        def step(i, carry):
            body(i)
            return carry
        lax.fori_loop(1, n, step, 0)

    barrier = pltpu.get_barrier_semaphore()
    each(16, lambda d: pl.semaphore_signal(barrier, inc=1, device_id=(d_peer(d), t), device_id_type=MESH))
    each(16, lambda d: pl.semaphore_signal(barrier, inc=1, device_id=(dp, (t + d) % 16), device_id_type=MESH))

    copies = [
        pltpu.make_async_copy(tok_hbm, tok, ldma.at[0]),
        pltpu.make_async_copy(og_hbm, og, ldma.at[1]),
        pltpu.make_async_copy(warm_hbm, warm, ldma.at[2]),
    ]
    for copy in copies:
        copy.start()
    chunk_copies = []
    for ch, (start, width) in enumerate(BLOCKS):
        rows = pl.ds(start, width)
        group = [
            pltpu.make_async_copy(src.at[rows], dst.at[rows], cdma.at[i, ch])
            for i, (src, dst) in enumerate(((gate_hbm, gate), (up_hbm, up), (hid_hbm, hid)))
        ]
        for copy in group:
            copy.start()
        chunk_copies.append(group)

    copies[0].wait()
    copies[1].wait()
    keep = lax.broadcasted_iota(jnp.int32, (ROWS, DWP), 1) < DW
    for which, ref in enumerate((tok, og)):
        for g in range(16):
            first = (DW * g) // 128
            shift = DW * g - 128 * first
            width = 512 if shift <= 48 else 640
            wide = ref[:, 128 * first : 128 * first + width].astype(F32)
            if shift:
                wide = pltpu.roll(wide, width - shift, 1)
            apad[which, g] = jnp.where(keep, wide[:, :DWP], 0.0).astype(BF16)
    for copy in copies[2:]:
        copy.wait()

    lane = lax.broadcasted_iota(jnp.int32, (16, 128), 1)
    terms = [0.0, 0.0, 0.0]
    for ch, (start, width) in enumerate(BLOCKS):
        if ch == 2:
            pl.semaphore_wait(barrier, 30)

            def scatter_tokens(d):
                for which in range(2):
                    remote(apad.at[which, d_peer(d)], arecv.at[which, d], which, (d_peer(d), t)).start()

            each(16, scatter_tokens)
        for copy in chunk_copies[ch]:
            copy.wait()

        def swiglu(i, carry):
            rows = pl.ds(pl.multiple_of(start + i * 16, 16), 16)
            g = gate[rows, :].astype(F32)
            u = up[rows, :].astype(F32)
            h = hid[rows, :].astype(F32)
            s = 0.5 * jnp.tanh(0.5 * g) + 0.5
            silu = g * s
            slope = s * (1.0 + g * (1.0 - s))
            bmat[0, rows, :] = (h * u * slope).astype(BF16)
            bmat[1, rows, :] = (h * silu).astype(BF16)
            bmat[2, rows, :] = (silu * u).astype(BF16)
            return carry

        lax.fori_loop(0, width // 16, swiglu, 0, unroll=2)
        for k in range(3):
            terms[k] += dot(warm[k, :, start : start + width], bmat[k, start : start + width, :], NN)
    c01 = jnp.concatenate([terms[0], terms[1]], axis=0).T
    c22 = jnp.concatenate([terms[2], terms[2]], axis=0).T
    for i in range(16):
        cpart[i % 2, i // 2, 0:32, :] = c01[32 * i : 32 * i + 32]
        cpart[i % 2, i // 2, 32:48, :] = jnp.where(
            lane < 64, c22[32 * i : 32 * i + 16], c22[32 * i + 16 : 32 * i + 32]
        )

    sibling = (dp, 2 * z + 1 - c)
    remote(cpart.at[1 - c], csib, 2, sibling).start()
    arrived(csib, 2)
    csum[...] = cpart[c] + csib[...]
    each(8, lambda d: remote(csum.at[z_peer(d)], crecv.at[d], 3, (dp, 2 * z_peer(d) + c)).start())
    arrived(crecv.at[pl.ds(1, 7)], 3)
    total = csum[z]
    for d in range(1, 8):
        total = total + crecv[d]
    cgath[0] = total

    each(16, lambda d: remote(cgath.at[0], cgath.at[d], 4, (d_peer(d), t)).start())
    for which in range(2):
        arecv[which, 0] = apad[which, dp]
        arrived(arecv.at[which, pl.ds(1, 15)], which)
    arrived(cgath.at[pl.ds(1, 15)], 4)

    c01 = cgath[:, 0:32, :].reshape(GROUP, 128)
    fold = cgath[:, 32:48, :].reshape(256, 128)
    other = pltpu.roll(fold, 64, 1)
    c2 = jnp.concatenate([fold.reshape(16, 16, 128), other.reshape(16, 16, 128)], axis=1).reshape(GROUP, 128)
    atok = arecv[0].reshape(GROUP, DWP)
    aog = arecv[1].reshape(GROUP, DWP)
    high, low = split(c01.T)
    left01 = dot(high, atok, NN) + dot(low, atok, NN)
    high, low = split(c2.T[0:64])
    left2 = dot(high, aog, NN) + dot(low, aog, NN)
    for half in range(2):
        cols = slice(256 * half, 256 * half + 256)
        lpart[half, 0:128, :] = left01[:, cols]
        lpart[half, 128:192, :] = left2[:, cols]

    remote(lpart.at[1 - c], lsib, 5, sibling).start()
    arrived(lsib, 5)
    lsum[...] = (lpart[c] + lsib[...]).reshape(8, 24, 256)
    each(8, lambda d: remote(lsum.at[z_peer(d)], lrecv.at[d], 6, (dp, 2 * z_peer(d) + c)).start())
    arrived(lrecv.at[pl.ds(1, 7)], 6)
    total = lsum[z]
    for d in range(1, 8):
        total = total + lrecv[d]
    lfull[c, z] = total
    each(8, lambda d: remote(lfull.at[c, z], lfull.at[c, z], 7, (dp, 2 * z_peer(d) + c)).start())
    arrived(lrecv.at[pl.ds(1, 7)], 7)
    remote(lfull.at[c], lfull.at[c], 8, sibling).start()
    arrived(lsib, 8)

    left = jnp.concatenate([lfull[0].reshape(192, 256), lfull[1].reshape(192, 256)], axis=1)
    left01 = left[0:128]
    left2 = left[128:192]
    left22 = jnp.concatenate([left2, left2], axis=0)

    lane64 = lax.broadcasted_iota(jnp.int32, (64, 128), 1)
    gram01 = dot(left01, left01, NT, HIGHEST)
    gram22 = dot(left2, left22, NT, HIGHEST)
    gpart[0:4] = jnp.where(lane64 < 64, gram01[0:64], gram01[64:128]).reshape(4, 16, 128)
    gpart[4:8] = gram22.reshape(4, 16, 128)
    each(16, lambda d: remote(gpart.at[z], grecv.at[d], 10, (d_peer(d), t)).start())

    high, low = split(left01)
    u01 = dot(atok, high, NT) + dot(atok, low, NT)
    high, low = split(left22)
    u22 = (dot(aog, high, NT) + dot(aog, low, NT)).reshape(16, 32, 128)
    upart[:, 0:32, :] = u01.reshape(16, 32, 128)
    lane3 = lax.broadcasted_iota(jnp.int32, (16, 16, 128), 2)
    upart[:, 32:48, :] = jnp.where(lane3 < 64, u22[:, 0:16], u22[:, 16:32])
    each(16, lambda d: remote(upart.at[d], urecv.at[d], 9, (d_back(d), t)).start())

    arrived(grecv.at[pl.ds(1, 15)], 10)
    total = gpart[z]
    for d in range(1, 16):
        total = total + grecv[d]
    gfull[z] = total
    each(8, lambda d: remote(gfull.at[z], gfull.at[z], 11, (dp, 2 * z_peer(d) + c)).start())
    arrived(grecv.at[pl.ds(1, 7)], 11)

    packed = gfull[...].reshape(128, 128)
    pair = pltpu.roll(packed[0:64], 64, 1)
    row64 = lax.broadcasted_iota(jnp.int32, (64, 128), 0)
    unit = jnp.where(lane64 % 64 == row64, 1.0, 0.0)
    work = [
        jnp.where(lane64 < 64, unit, pair),
        jnp.where(lane64 < 64, pair, unit),
        jnp.where(lane64 < 64, unit, packed[64:128]),
    ]
    place = (64, 0, 64)
    for j in range(63):
        top = (j // 8) * 8
        for k in range(3):
            m = work[k]
            pivot_row = m[j : j + 1, :]
            at = place[k] + j
            scaled = pivot_row * (1.0 / m[j : j + 1, at : at + 1])
            below = m[top:, :]
            column = jnp.where(row64[top:, :] > j, below[:, at : at + 1], 0.0)
            below = below - column * scaled
            work[k] = below if top == 0 else jnp.concatenate([m[:top], below], axis=0)
    inverse = []
    for k in range(3):
        m = work[k]
        diagonal = jnp.sum(jnp.where(lane64 == row64 + place[k], m, 0.0), axis=1, keepdims=True)
        m = m * lax.rsqrt(diagonal)
        inverse.append(jnp.where((lane64 < 64) == (place[k] == 64), m, 0.0))
    bd01 = jnp.concatenate([inverse[0], inverse[1]], axis=0)
    bd22 = jnp.concatenate([inverse[2], pltpu.roll(inverse[2], 64, 1)], axis=0)

    arrived(urecv.at[pl.ds(1, 15)], 9)
    total = upart[0]
    for d in range(1, 16):
        total = total + urecv[d]
    proj = jnp.concatenate(
        [dot(total[0:32], bd01, NT, HIGHEST), dot(total[32:48], bd22, NT, HIGHEST)], axis=0
    ).astype(BF16)
    pgath[c, z] = proj
    each(8, lambda d: remote(pgath.at[c, z], pgath.at[c, z], 12, (dp, 2 * z_peer(d) + c)).start())

    owner_x, owner_y = t // 4, t % 4

    @pl.when(dp == t)
    def _():
        lout[0:128, :] = dot(bd01, left01, NN, HIGHEST).astype(BF16)
        lout[128:192, :] = dot(bd22[0:64], left22, NN, HIGHEST).astype(BF16)
        each(4, lambda d: remote(lout, lout, 14, (((x + d) % 4) * 4 + y, t)).start())

    arrived(pgath.at[c, pl.ds(0, 7)], 12)
    remote(pgath.at[c], pgath.at[c], 13, sibling).start()
    arrived(pgath.at[c], 13)

    @pl.when(jnp.logical_and(y == owner_y, x != owner_x))
    def _():
        arrived(lout, 14)

    @pl.when(y == owner_y)
    def _():
        each(4, lambda d: remote(lout, lout, 15, (x * 4 + (y + d) % 4, t)).start())

    whole = jnp.concatenate([pgath[i % 2, i // 2, 0:32, :] for i in range(16)], axis=0).astype(F32)
    parts = []
    for i in range(16):
        fold = pgath[i % 2, i // 2, 32:48, :].astype(F32)
        parts += [fold, pltpu.roll(fold, 64, 1)]
    p01 = whole.T.astype(BF16)
    p2 = jnp.concatenate(parts, axis=0).T.astype(BF16)
    lhs = (p01[0:64], p01[64:128], p2[0:64])
    for h, (start, width) in enumerate(HALVES):
        terms = [dot(lhs[k], bmat[k, start : start + width, :], NT).astype(BF16) for k in range(3)]
        both = jnp.concatenate(terms, axis=0)
        for i in range(4):
            for j in range(4):
                size = min(PIECE, width - PIECE * j)
                if size > 0:
                    rpart[h, 4 * i + j, :, 0:size] = both[48 * i : 48 * i + 48, PIECE * j : PIECE * j + size]
        each(16, lambda d: remote(rpart.at[h, d_peer(d)], rrecv.at[h, d], 16 + h, (d_peer(d), t)).start())

    for h, (start, width) in enumerate(HALVES):
        arrived(rrecv.at[h, pl.ds(1, 15)], 16 + h)
        own_cols = pl.ds(pl.multiple_of(start + y * PIECE, PIECE), PIECE)
        for r in range(3):
            rows = slice(16 * r, 16 * r + 16)
            total = rpart[h, dp, rows, :].astype(F32)
            for d in range(1, 16):
                total = total + rrecv[h, d, rows, :].astype(F32)
            rgath[pl.ds(pl.multiple_of(x * 48 + 16 * r, 16), 16), own_cols] = (total * (1.0 / 16)).astype(BF16)
        own = rgath.at[pl.ds(pl.multiple_of(x * 48, 16), 48), own_cols]
        each(16, lambda d: remote(own, own, 16 + SPLITS + h, (d_peer(d), t)).start())

    @pl.when(y != owner_y)
    def _():
        arrived(lout, 15)

    out_left[...] = lout[:, 0:DW]
    for h, (start, width) in enumerate(HALVES):
        arrived(rrecv.at[h, pl.ds(1, 15)], 16 + SPLITS + h)
        out_right[:, start : start + width] = rgath[:, start : start + width]

    for which in range(2):
        sent(arecv.at[which, pl.ds(1, 15)], which)
    sent(csib, 2)
    sent(crecv.at[pl.ds(1, 7)], 3)
    sent(cgath.at[pl.ds(1, 15)], 4)
    sent(lsib, 5)
    sent(lrecv.at[pl.ds(1, 7)], 6)
    sent(lrecv.at[pl.ds(1, 7)], 7)
    sent(lsib, 8)
    sent(urecv.at[pl.ds(1, 15)], 9)
    sent(grecv.at[pl.ds(1, 15)], 10)
    sent(grecv.at[pl.ds(1, 7)], 11)
    sent(pgath.at[0, pl.ds(0, 7)], 12)
    sent(pgath.at[0], 13)

    @pl.when(dp == t)
    def _():
        each(4, lambda d: sent(lout, 14))

    @pl.when(y == owner_y)
    def _():
        each(4, lambda d: sent(lout, 15))

    for h in range(2 * SPLITS):
        sent(rrecv.at[0, pl.ds(1, 15)], 16 + h)


def shards(tokens, out_grad, gate_pre, up_pre, hidden_grad, warm_basis):
    vmem = pltpu.VMEM
    scratch = [
        vmem((ROWS, 7424), BF16), vmem((ROWS, 7424), BF16),
        vmem((FFW, GROUP), BF16), vmem((FFW, GROUP), BF16), vmem((FFW, GROUP), BF16),
        vmem((3, 64, FFW), BF16),
        vmem((2, 16, ROWS, DWP), BF16), vmem((2, 16, ROWS, DWP), BF16),
        vmem((3, FFW, GROUP), BF16),
        vmem((2, 8, 48, 128), F32), vmem((8, 48, 128), F32), vmem((8, 48, 128), F32),
        vmem((8, 48, 128), F32), vmem((16, 48, 128), F32),
        vmem((2, 192, 256), F32), vmem((192, 256), F32), vmem((8, 24, 256), F32),
        vmem((8, 24, 256), F32), vmem((2, 8, 24, 256), F32),
        vmem((16, 48, 128), F32), vmem((16, 48, 128), F32),
        vmem((8, 16, 128), F32), vmem((16, 16, 128), F32), vmem((8, 16, 128), F32),
        vmem((2, 8, 48, 128), BF16), vmem((192, DWP), BF16),
        vmem((SPLITS, 16, 48, PIECE), BF16), vmem((SPLITS, 16, 48, PIECE), BF16), vmem((192, 2048), BF16),
        pltpu.SemaphoreType.DMA((3,)), pltpu.SemaphoreType.DMA((3, 4)),
        pltpu.SemaphoreType.DMA((16 + 2 * SPLITS,)), pltpu.SemaphoreType.DMA((16 + 2 * SPLITS,)),
    ]
    left, right = pl.pallas_call(
        kernel,
        out_shape=(jax.ShapeDtypeStruct((192, DW), BF16), jax.ShapeDtypeStruct((192, FFW), BF16)),
        in_specs=[pl.BlockSpec(memory_space=pl.ANY)] * 6,
        out_specs=(pl.BlockSpec(memory_space=pltpu.VMEM), pl.BlockSpec(memory_space=pltpu.VMEM)),
        scratch_shapes=scratch,
        compiler_params=pltpu.CompilerParams(
            collective_id=0, has_side_effects=True, vmem_limit_bytes=60 * 2**20
        ),
    )(tokens, out_grad, gate_pre.T, up_pre.T, hidden_grad.T, warm_basis)
    return left.astype(F32).reshape(3, 64, DW), right.astype(F32).reshape(3, 64, FFW)


def solution(mesh):
    placed = (
        P(("dp", "tensor"), None),
        P(("dp", "tensor"), None),
        P("dp", "tensor"),
        P("dp", "tensor"),
        P("dp", "tensor"),
        P(None, None, "tensor"),
    )
    return jax.shard_map(
        shards,
        mesh=mesh,
        in_specs=placed,
        out_specs=(P(None, None, "tensor"), P(None, None, "tensor")),
        check_vma=False,
    )
```
